32 devices in a mesh: exp: 4 (over z), row: 4 (over y, x), col: 2 (over core).
Axes of the slice: x: 2, y: 2, z: 4, core: 2. Of those that a mesh axis runs over, the one named last changes fastest.
Arguments:
- tokens: bfloat16 [4096, 768], P(('exp', 'col')), may hold values from -6 to 6
- qkv_weight: bfloat16 [3, 768, 768], P(None, ('exp', 'col'), 'row'), may hold values from -0.21875 to 0.21875
- out_weight: bfloat16 [768, 768], P('row', ('exp', 'col')), may hold values from -1.25 to 1.25
- bias_table: bfloat16 [32, 12], P(None, 'row'), may hold values from -4 to 4
- gain_attn: bfloat16 [768], P(('exp', 'col')), may hold values from 0.5 to 1.5
- gain_expert: bfloat16 [768], P(('exp', 'col')), may hold values from 0.5 to 1.5
- router_weight: bfloat16 [768, 8], P(('exp', 'col')), may hold values from -0.15625 to 0.15625
- expert_in: bfloat16 [8, 768, 3072], P(('exp', 'col'), None, 'row'), may hold values from -0.21875 to 0.21875
- expert_out: bfloat16 [8, 3072, 768], P(('exp', 'col'), 'row'), may hold values from -6 to 6
- lengths: int32 [8], P(('exp', 'col')), may hold values from 1 to 512, 3072 in all
- routes: int32 [4096, 1], P(('exp', 'col')), may hold values from 0 to 7
- cotangent: bfloat16 [4096, 768], P(('exp', 'col')), may hold values from -6 to 6
Outputs:
- result: bfloat16 [4096, 768], P(('exp', 'col'))
- grad_tokens: bfloat16 [4096, 768], P(('exp', 'col'))
- grad_qkv_weight: float32 [3, 768, 768], P(None, ('exp', 'col'), 'row')
- grad_out_weight: float32 [768, 768], P('row', ('exp', 'col'))
- grad_bias_table: float32 [32, 12], P(None, 'row')
- grad_gain_attn: float32 [768], P(('exp', 'col'))
- grad_gain_expert: float32 [768], P(('exp', 'col'))
- grad_router: float32 [768, 8], P(('exp', 'col'))
- grad_expert_in: float32 [8, 768, 3072], P(('exp', 'col'), None, 'row')
- grad_expert_out: float32 [8, 3072, 768], P(('exp', 'col'), 'row')
The draws below stay inside these ranges and needn't reach their ends.
All inputs are finite; a program needn't handle non-finite values. No bound on the sum of `lengths` on one device may be relied on, other than what follows from the above.
Results may differ from the reference program's by a relative error of at most 0.015.
Values may be sent and summed in bfloat16 or wider, within the bound.
A program may use at most 128 MiB of HBM per device.

```python
import math
import jax
import jax.numpy as jnp
import numpy as np
from jax import lax

D = 768
HEADS = 12
DH = 64
FF = 3072
BUCKETS = 32
LMAX = 512
WIN_DEV = 1
CAP = 8
EXPERTS = 8
NSEQ = 8
TOKENS = 4096


def shard_levels(key, shape, cuts, smallest, top_value):
    factor_of = 1.0
    for axis_at, parts in cuts:
        draws = jax.random.uniform(jax.random.fold_in(jax.random.fold_in(key, 6), axis_at), (parts,), jnp.float32, smallest / len(cuts), top_value / len(cuts))
        factor_of = factor_of * jnp.repeat(jnp.exp(draws), shape[axis_at] // parts).reshape((-1,) + (1,) * (len(shape) - 1 - axis_at))
    return factor_of


def different_ones(key, rows, number_of, top, lift):
    ranking = jax.random.permutation(jax.random.fold_in(key, 1), number_of)
    pull = ranking
    for power in range(3):
        pull = pull * pull // number_of
    pull = pull * lift // number_of
    tickets = jax.random.randint(jax.random.fold_in(key, 2), (rows, number_of), 0, 4096) + pull
    holders = jax.random.permutation(jax.random.fold_in(key, 3), rows)[jnp.arange(number_of) % rows]
    tickets = jnp.where(jnp.arange(rows)[:, None] == holders[None, :], 1 << 14, tickets)
    score = tickets * number_of + jnp.arange(number_of)
    return lax.top_k(score.astype(jnp.int32), top)[1].astype(jnp.int32)


def split_up(count, total, limit, skew):
    portions = [(1 << 20) // math.isqrt(rank ** skew) + 1 for rank in range(2, count + 1)]
    surplus, given = total - limit - (count - 1), [1] * (count - 1)
    while surplus > 0:
        candidates = [i for i in range(count - 1) if given[i] < limit]
        pool, budget = sum([portions[i] for i in candidates]), surplus
        for i in candidates:
            addition = min(limit - given[i], max(1, budget * portions[i] // pool), surplus)
            given[i] = given[i] + addition
            surplus = surplus - addition
    return np.array([limit] + given)


def uneven_parts(key, number_of, total, limit, lean):
    if number_of == 2:
        one = jax.random.randint(key, (), max(1, total - limit), min(limit, total - 1) + 1)
        return jnp.stack([one, total - one])
    sizes = jnp.asarray(split_up(number_of, total, limit, lean), jnp.int32)
    couples = (number_of - 1) // 2
    source_of, receiver = sizes[1:1 + 2 * couples:2], sizes[2:2 + 2 * couples:2]
    margin = jnp.minimum(source_of - 1, limit - receiver)
    moved = jax.random.randint(jax.random.fold_in(key, 1), (couples,), 0, 1 << 20) % (margin + 1)
    sizes = sizes.at[1:1 + 2 * couples:2].set(source_of - moved).at[2:2 + 2 * couples:2].set(receiver + moved)
    return sizes[jax.random.permutation(jax.random.fold_in(key, 2), number_of)]


def centred(own_key, dims, spread, most, cuts=(), kind=jnp.bfloat16):
    values = spread * jax.random.normal(own_key, dims, jnp.float32)
    if cuts:
        values = values * shard_levels(own_key, dims, cuts, -0.22, 0.18)
    return jnp.clip(values, -most, most).astype(kind)


def setup_inputs(seed: int = 0) -> dict:
    arg_keys = jax.random.split(jax.random.key(seed), 13)
    tokens = centred(arg_keys[0], (TOKENS, D), 1.0, 6.0, ((0, 8),))
    qkv_weight = centred(arg_keys[1], (3, D, D), D ** -0.5, 0.21875, ((1, 8), (2, 4)))
    out_weight = centred(arg_keys[2], (D, D), (D // 32) ** -0.5, 1.25, ((0, 4), (1, 8)))
    bias_table = centred(arg_keys[3], (BUCKETS, HEADS), 1.0, 4.0, ((1, 4),))
    gain_attn = jnp.clip(1.0 + 0.1 * jax.random.normal(arg_keys[4], (D,), jnp.float32), 0.5, 1.5).astype(jnp.bfloat16)
    gain_expert = jnp.clip(1.0 + 0.1 * jax.random.normal(arg_keys[5], (D,), jnp.float32), 0.5, 1.5).astype(jnp.bfloat16)
    router_weight = centred(arg_keys[6], (D, EXPERTS), (2 * D) ** -0.5, 0.15625, ((0, 8),))
    expert_in = centred(arg_keys[7], (EXPERTS, D, FF), D ** -0.5, 0.21875, ((0, 8), (2, 4)))
    expert_out = centred(arg_keys[8], (EXPERTS, FF, D), (max(FF // 3072, 1)) ** -0.5, 6.0, ((0, 8), (1, 4)))
    lengths = uneven_parts(arg_keys[9], NSEQ, 3 * LMAX * NSEQ // 4, LMAX, 2).astype(jnp.int32)
    routes = different_ones(arg_keys[10], TOKENS, EXPERTS, 1, 1024)
    cotangent = centred(arg_keys[11], (TOKENS, D), 1.0, 6.0, ((0, 8),))
    return dict(tokens=tokens, qkv_weight=qkv_weight, out_weight=out_weight, bias_table=bias_table, gain_attn=gain_attn, gain_expert=gain_expert, router_weight=router_weight, expert_in=expert_in, expert_out=expert_out, lengths=lengths, routes=routes, cotangent=cotangent)


epsilon = 1e-06
thresholds = np.array([12, 16, 23, 32, 46, 64, 91], dtype=np.int32)
highest = lax.Precision.HIGHEST

@jax.custom_vjp
def low(v):
    return lax.optimization_barrier(v.astype(jnp.bfloat16)).astype(jnp.float32)

@jax.custom_vjp
def low_back(v):
    return v

def low_keep(v):
    return (low(v), None)

def low_pass(kept, grad):
    return (grad,)

def back_keep(v):
    return (v, None)

def back_low(kept, grad):
    return (low(grad),)
low.defvjp(low_keep, low_pass)
low_back.defvjp(back_keep, back_low)

def bucket_of(offset):
    distance = jnp.abs(offset)
    beyond = lax.optimization_barrier(jnp.sum((distance[..., None] >= jnp.asarray(thresholds)).astype(jnp.int32), axis=-1)).astype(jnp.int32)
    return (offset > 0).astype(jnp.int32) * 16 + jnp.minimum(distance, 8) + beyond

def rms_norm(values, gain_row):
    return values * lax.rsqrt(lax.optimization_barrier(jnp.mean(values * values, axis=-1, keepdims=True)) + epsilon) * gain_row

def routing(lengths, routes):
    position = jnp.arange(TOKENS, dtype=jnp.int32)
    block_len = WIN_DEV * LMAX
    is_live = position % LMAX < lengths[position // LMAX]
    chosen = routes[:, 0]
    route_hot = chosen[:, None] == jnp.arange(EXPERTS, dtype=jnp.int32)[None, :]
    live_hot = (route_hot & is_live[:, None]).astype(jnp.int32).reshape(TOKENS // block_len, block_len, EXPERTS)
    earlier = (jnp.cumsum(live_hot, axis=1).astype(jnp.int32) - live_hot).reshape(TOKENS, EXPERTS)
    slot_rank = lax.optimization_barrier(jnp.sum(jnp.where(route_hot, earlier, 0), axis=-1)).astype(jnp.int32)
    is_kept = is_live & (slot_rank < CAP)
    target = jnp.where(is_kept, chosen * CAP + slot_rank, 0).astype(jnp.int32)
    return (route_hot, position // block_len, target, is_kept)

def reference(tokens, qkv_weight, out_weight, bias_table, gain_attn, gain_expert, router_weight, expert_in, expert_out, lengths, routes, cotangent):
    route_hot, device, target, is_kept = routing(lengths, routes)
    block_count = TOKENS // (WIN_DEV * LMAX)
    seq_group = math.gcd(NSEQ, max(1, 4096 // LMAX))
    place = jnp.arange(LMAX, dtype=jnp.int32)
    buckets = bucket_of(place[None, :] - place[:, None])
    seq_lens = lengths.reshape(NSEQ // seq_group, seq_group)
    drop_target = jnp.where(is_kept, target, EXPERTS * CAP).astype(jnp.int32)

    def forward(token_rows, qkv_w, out_w, table, gain_one, gain_two, router_w, first_weight, second_weight):
        normed_one = low(rms_norm(token_rows, gain_one))
        projected = low(low_back(jnp.einsum('td,sde->ste', normed_one, qkv_w, precision=highest)))
        bias_grid = jnp.transpose(table[buckets], (2, 0, 1))

        def split(part):
            return part.reshape(NSEQ // seq_group, seq_group, LMAX, HEADS, DH)

        def attend(pieces):
            query_part, key_part, value_part, lens_part = pieces
            score_grid = jnp.einsum('gqhd,gkhd->ghqk', query_part, key_part, precision=highest) * DH ** (-0.5) + bias_grid[None]
            score_grid = low_back(score_grid)
            key_valid = place[None, :] < lens_part[:, None]
            score_grid = jnp.where(key_valid[:, None, None, :], score_grid, -1e+30)
            row_max = lax.optimization_barrier(jnp.max(score_grid, axis=-1, keepdims=True))
            exp_scores = jnp.exp(score_grid - row_max)
            prob_low = low(exp_scores / lax.optimization_barrier(jnp.sum(exp_scores, axis=-1, keepdims=True)))
            return jnp.einsum('ghqk,gkhd->gqhd', prob_low, value_part, precision=highest)
        attended = lax.map(jax.checkpoint(attend), (split(projected[0]), split(projected[1]), split(projected[2]), seq_lens))
        heads_low = low(low_back(attended.reshape(TOKENS, D)))
        attn = low_back(jnp.dot(heads_low, out_w, precision=highest))
        mixed = token_rows + attn
        normed_two = low(rms_norm(mixed, gain_two))
        router_probs = jax.nn.softmax(jnp.dot(normed_two, router_w, precision=highest), axis=-1)
        gate_prob = lax.optimization_barrier(jnp.sum(jnp.where(route_hot, router_probs, 0.0), axis=-1))
        buffer = jnp.zeros((block_count, EXPERTS * CAP, D), jnp.float32)
        buffer = buffer.at[device, drop_target].add(jnp.where(is_kept[:, None], normed_two, 0.0), mode='drop')
        grouped = buffer.reshape(block_count, EXPERTS, CAP, D).transpose(1, 0, 2, 3).reshape(EXPERTS, block_count * CAP, D)

        def expert(pieces):
            slot_rows, weight_a, weight_b = pieces
            before_act = low_back(jnp.dot(slot_rows, weight_a, precision=highest))
            hidden = low(jax.nn.gelu(before_act))
            return low_back(jnp.dot(hidden, weight_b, precision=highest))
        answers = lax.map(jax.checkpoint(expert), (grouped, first_weight, second_weight))
        answers = answers.reshape(EXPERTS, block_count, CAP, D).transpose(1, 0, 2, 3).reshape(block_count, EXPERTS * CAP, D)
        returned = jnp.where(is_kept[:, None], answers[device, target], 0.0)
        return mixed + gate_prob[:, None] * returned
    floats = tuple((a.astype(jnp.float32) for a in (tokens, qkv_weight, out_weight, bias_table, gain_attn, gain_expert, router_weight, expert_in, expert_out)))
    result, pullback = jax.vjp(forward, *floats)
    gradients = pullback(cotangent.astype(jnp.float32))
    return (result.astype(jnp.bfloat16), gradients[0].astype(jnp.bfloat16), gradients[1], gradients[2], gradients[3], gradients[4], gradients[5], gradients[6], gradients[7], gradients[8])
```

```python
import functools

import jax
import jax.numpy as jnp
import numpy as np
from jax import lax
from jax.experimental import pallas as pl
from jax.experimental.pallas import tpu as pltpu
from jax.sharding import PartitionSpec as P

DH = 64
CAP = 8
F32 = jnp.float32
BF16 = jnp.bfloat16
epsilon = 1e-06
thresholds = np.array([12, 16, 23, 32, 46, 64, 91], dtype=np.int32)
highest = lax.Precision.HIGHEST
MESH = pl.DeviceIdType.MESH
LIMIT = 56 * 1024 * 1024
VMEM = pl.BlockSpec(memory_space=pltpu.VMEM)
SMEM = pl.BlockSpec(memory_space=pltpu.SMEM)


def nt(a, b, precision=None):
    return lax.dot_general(
        a, b, (((1,), (1,)), ((), ())), preferred_element_type=F32, precision=precision
    )


def tn(a, b, precision=None):
    return lax.dot_general(
        a, b, (((0,), (0,)), ((), ())), preferred_element_type=F32, precision=precision
    )


def nn(a, b, precision=None):
    return jnp.dot(a, b, preferred_element_type=F32, precision=precision)


def call(kernel, outs, args, scratch=(), collective=None, specs=None):
    params = dict(vmem_limit_bytes=LIMIT)
    if collective is not None:
        params.update(collective_id=collective, has_side_effects=True)
    return pl.pallas_call(
        kernel,
        out_shape=[jax.ShapeDtypeStruct(s, d) for s, d in outs],
        in_specs=specs or [VMEM] * len(args),
        out_specs=[VMEM] * len(outs),
        scratch_shapes=list(scratch),
        compiler_params=pltpu.CompilerParams(**params),
    )(*args)


def enter(peers):
    barrier = pltpu.get_barrier_semaphore()
    for peer in peers:
        pl.semaphore_signal(barrier, inc=1, device_id=peer, device_id_type=MESH)
    pl.semaphore_wait(barrier, len(peers))


def remote(src, dst, send, recv, peer):
    copy = pltpu.make_async_remote_copy(
        src_ref=src, dst_ref=dst, send_sem=send, recv_sem=recv, device_id=peer, device_id_type=MESH
    )
    copy.start()
    return copy


def ring(axis, size):
    me = lax.axis_index(axis)
    return [lax.rem(me + k, size) for k in range(1, size)]


def group_peers(n_exp, n_col):
    n = n_exp * n_col
    me = lax.axis_index("exp") * n_col + lax.axis_index("col")
    return [lax.rem(me + k, n) for k in range(1, n)]


def gather_kernel(n_exp, w, s, w_all, s_all, send, recv, send_s, recv_s, c_send, c_recv, d_send, d_recv):
    e = lax.axis_index("exp")
    c = lax.axis_index("col")
    other = {"col": 1 - c}
    peers = ring("exp", n_exp)
    enter([{"exp": p} for p in peers] + [other])
    copies = []
    for k, p in enumerate(peers):
        copies.append(remote(s, s_all.at[e, c], send_s.at[k], recv_s.at[k], {"exp": p}))
        copies.append(remote(w, w_all.at[e, c], send.at[k], recv.at[k], {"exp": p}))
    last = [
        remote(s, s_all.at[e, c], d_send.at[0], d_recv.at[0], other),
        remote(w, w_all.at[e, c], c_send.at[0], c_recv.at[0], other),
    ]
    w_all[e, c] = w[...]
    s_all[e, c] = s[...]
    for k in range(n_exp - 1):
        q = lax.rem(e + n_exp - k - 1, n_exp)
        copies[2 * k].wait_recv()
        last.append(remote(s_all.at[q, c], s_all.at[q, c], d_send.at[k + 1], d_recv.at[k + 1], other))
        copies[2 * k + 1].wait_recv()
        last.append(remote(w_all.at[q, c], w_all.at[q, c], c_send.at[k + 1], c_recv.at[k + 1], other))
    for copy in copies:
        copy.wait_send()
    for copy in last:
        copy.wait()


def row_sum_kernel(n_row, x, out, held, send, recv, send2, recv2):
    r = lax.axis_index("row")
    peers = ring("row", n_row)
    enter([{"row": p} for p in peers])
    copies = [
        remote(x.at[p], held.at[k], send.at[k], recv.at[k], {"row": p}) for k, p in enumerate(peers)
    ]
    total = x[r].astype(F32)
    for k, copy in enumerate(copies):
        copy.wait_recv()
        total = total + held[k].astype(F32)
    out[r] = total.astype(BF16)
    more = [
        remote(out.at[r], out.at[r], send2.at[k], recv2.at[k], {"row": p})
        for k, p in enumerate(peers)
    ]
    for copy in copies:
        copy.wait_send()
    for copy in more:
        copy.wait()


def dispatch_kernel(n_exp, n_col, x, out, send, recv):
    me = lax.axis_index("exp") * n_col + lax.axis_index("col")
    peers = group_peers(n_exp, n_col)
    ids = [{"exp": p // n_col, "col": lax.rem(p, n_col)} for p in peers]
    enter(ids)
    copies = [
        remote(x.at[p], out.at[me], send.at[k], recv.at[k], ids[k]) for k, p in enumerate(peers)
    ]
    out[me] = x[me]
    for copy in copies:
        copy.wait()


def return_kernel(n_exp, n_col, n_row, x, out, held, total, send, recv, send2, recv2):
    n = n_exp * n_col
    share = n // n_row
    e = lax.axis_index("exp")
    c = lax.axis_index("col")
    r = lax.axis_index("row")
    me = e * n_col + c
    peers = ring("row", n_row)
    targets = []
    for g in range(share):
        for b in range(n_row):
            t = r * share + g
            targets.append((g, {"exp": t // n_col, "col": lax.rem(t, n_col), "row": b}))
    mine = me // share == r
    everyone = [
        (lax.rem(r + b, n_row), lax.rem(me + k, n))
        for b in range(n_row)
        for k in range(n)
        if b or k
    ]
    enter([{"exp": k // n_col, "col": lax.rem(k, n_col), "row": b} for b, k in everyone])
    copies = [
        remote(
            x.at[pl.ds(p * share, share)], held.at[k], send.at[k], recv.at[k], {"row": p}
        )
        for k, p in enumerate(peers)
    ]
    acc = x[pl.ds(r * share, share)].astype(F32)
    for k, copy in enumerate(copies):
        copy.wait_recv()
        acc = acc + held[k].astype(F32)
    total[...] = acc.astype(BF16)
    started = []
    for k, (g, target) in enumerate(targets):
        own = mine & (r * share + g == me) & (target["row"] == r)
        copy = pltpu.make_async_remote_copy(
            src_ref=total.at[g],
            dst_ref=out.at[me],
            send_sem=send2.at[k],
            recv_sem=recv2.at[me],
            device_id=target,
            device_id_type=MESH,
        )

        @pl.when(own)
        def _(g=g):
            out[me] = total[g]

        @pl.when(jnp.logical_not(own))
        def _(copy=copy):
            copy.start()

        started.append((own, copy))

    for own, copy in started:

        @pl.when(jnp.logical_not(own))
        def _(copy=copy):
            copy.wait_send()

    for copy in copies:
        copy.wait_send()
    for k in range(n):

        @pl.when(jnp.logical_not((k == me) & mine))
        def _(k=k):
            pltpu.make_async_remote_copy(
                src_ref=total.at[0],
                dst_ref=out.at[k],
                send_sem=send2.at[0],
                recv_sem=recv2.at[k],
                device_id={"row": r},
                device_id_type=MESH,
            ).wait_recv()


def final_kernel(
    n_exp, n_col, n_row, gw, sm, gh, tok, gm, gain,
    gt, gwo, smo,
    hrow, sib, pre, zheld, smheld, smrow,
    s_row, r_row, s_row2, r_row2, s_sib, r_sib, s_z, r_z, s_sm, r_sm, s_sm2, r_sm2,
):
    e = lax.axis_index("exp")
    c = lax.axis_index("col")
    r = lax.axis_index("row")
    me = e * n_col + c
    rows = ring("row", n_row)
    exps = ring("exp", n_exp)
    group = group_peers(n_exp, n_col)
    ids = [{"exp": p // n_col, "col": lax.rem(p, n_col)} for p in group]
    other = {"col": 1 - c}
    enter([{"row": p} for p in rows] + ids)
    sibling = remote(gw.at[1 - c], sib, s_sib, r_sib, other)
    row_copies = [
        remote(gh.at[p], hrow.at[k], s_row.at[k], r_row.at[k], {"row": p}) for k, p in enumerate(rows)
    ]
    small = [
        remote(sm.at[p], smheld.at[k], s_sm.at[k], r_sm.at[k], ids[k]) for k, p in enumerate(group)
    ]
    sibling.wait_recv()
    pre[...] = (gw[c].astype(F32) + sib[...].astype(F32)).astype(BF16)
    z_copies = [
        remote(pre.at[p], zheld.at[k], s_z.at[k], r_z.at[k], {"exp": p}) for k, p in enumerate(exps)
    ]
    part = sm[me]
    for k, copy in enumerate(small):
        copy.wait_recv()
        part = part + smheld[k]
    smrow[0] = part
    small2 = [
        remote(smrow.at[0], smrow.at[k + 1], s_sm2.at[k], r_sm2.at[k], {"row": p})
        for k, p in enumerate(rows)
    ]
    total = gh[r].astype(F32)
    for k, copy in enumerate(row_copies):
        copy.wait_recv()
        total = total + hrow[k].astype(F32)
    rows_in = tok[r].astype(F32)
    inv = lax.rsqrt(jnp.mean(rows_in * rows_in, axis=-1, keepdims=True) + epsilon)
    unit = rows_in * inv
    scaled = total * gain[...]
    grad = gm[r] + inv * (scaled - unit * jnp.mean(scaled * unit, axis=-1, keepdims=True))
    gt[r] = grad.astype(BF16)
    row_copies2 = [
        remote(gt.at[r], gt.at[r], s_row2.at[k], r_row2.at[k], {"row": p}) for k, p in enumerate(rows)
    ]
    full = part[9:10]
    for k, copy in enumerate(small2):
        copy.wait_recv()
        full = full + smrow[k + 1][9:10]
    row_at = lax.broadcasted_iota(jnp.int32, part.shape, 0)
    smo[...] = jnp.where(row_at == 9, jnp.broadcast_to(full, part.shape), part)
    wsum = pre[e].astype(F32)
    for k, copy in enumerate(z_copies):
        copy.wait_recv()
        wsum = wsum + zheld[k].astype(F32)
    gwo[...] = wsum
    for copy in [sibling] + row_copies + small + z_copies + small2:
        copy.wait_send()
    for copy in row_copies2:
        copy.wait()


def head_scores(q, k, rel_row, length, heads_at):
    size = q.shape[0]
    x = jnp.broadcast_to(rel_row, (size, 2 * size))
    bias = pltpu.roll(x, size + 1, 1, stride=1, stride_axis=0)[:, :size]
    scores = nt(q, k) * DH ** (-0.5) + bias
    key_at = lax.broadcasted_iota(jnp.int32, (1, size), 1)
    scores = jnp.where(key_at < length, scores, -1e30)
    top = jnp.max(scores, axis=-1, keepdims=True)
    raised = jnp.exp(scores - top)
    return raised * (1.0 / jnp.sum(raised, axis=-1, keepdims=True))


def forward_kernel(length, tok, w, gain, rel, hid, qkv, heads, attn):
    rows_in = tok[...].astype(F32)
    inv = lax.rsqrt(jnp.mean(rows_in * rows_in, axis=-1, keepdims=True) + epsilon)
    hid[...] = (rows_in * inv * gain[...]).astype(BF16)
    for m in range(3):
        qkv[m] = nn(hid[...], w[m]).astype(BF16)
    size = tok.shape[0]
    for h in range(qkv.shape[2] // DH):
        at = slice(h * DH, (h + 1) * DH)
        probs = head_scores(qkv[0, :, at], qkv[1, :, at], rel[h : h + 1], length[0], h)
        heads[:, at] = nn(probs.astype(BF16), qkv[2, :, at]).astype(BF16)
    attn[...] = nt(heads[...], w[3]).astype(BF16)


def middle(length, tok, attn, gain, router, route_row, route_col):
    size = tok.shape[0]
    experts = router.shape[0]
    mixed = tok[...].astype(F32) + attn[...].astype(F32)
    inv = lax.rsqrt(jnp.mean(mixed * mixed, axis=-1, keepdims=True) + epsilon)
    unit = mixed * inv
    hidden = (unit * gain[...]).astype(BF16)
    logits = nt(hidden, router[...])
    top = jnp.max(logits, axis=-1, keepdims=True)
    raised = jnp.exp(logits - top)
    probs = raised / jnp.sum(raised, axis=-1, keepdims=True)
    hot_col = lax.broadcasted_iota(jnp.int32, (size, experts), 1) == route_col[...]
    gate = jnp.sum(jnp.where(hot_col, probs, 0.0), axis=-1, keepdims=True)
    live = lax.broadcasted_iota(jnp.int32, (1, size), 1) < length
    hot = (lax.broadcasted_iota(jnp.int32, (experts, size), 0) == route_row[...]) & live
    hot = jnp.where(hot, 1.0, 0.0)
    earlier = jnp.where(
        lax.broadcasted_iota(jnp.int32, (size, size), 0)
        < lax.broadcasted_iota(jnp.int32, (size, size), 1),
        1.0,
        0.0,
    )
    before = nn(hot.astype(BF16), earlier.astype(BF16))
    rank = jnp.sum(hot * before, axis=0, keepdims=True).astype(jnp.int32)
    kept = live & (rank < CAP)
    target = jnp.where(kept, route_row[...] * CAP + rank, -1)
    match = lax.broadcasted_iota(jnp.int32, (experts * CAP, size), 0) == target
    match = jnp.where(match, 1.0, 0.0).astype(BF16)
    return mixed, inv, unit, hidden, probs, hot_col, gate, match


def send_kernel(length, tok, attn, gain, router, route_row, route_col, cot, out):
    _, _, _, hidden, _, _, gate, match = middle(
        length[0], tok, attn, gain, router, route_row, route_col
    )
    grad = (gate * cot[...].astype(F32)).astype(BF16)
    n = out.shape[0]
    first = nn(match, hidden).reshape(n, CAP, -1)
    second = nn(match, grad).reshape(n, CAP, -1)
    out[...] = jnp.concatenate([first, second], axis=1).astype(BF16)


def expert_kernel(x, w_in, w_out, part, grad_in, grad_out):
    n = x.shape[0]
    both = x[...].astype(F32)
    rows = both[:, :CAP].reshape(n * CAP, -1).astype(BF16)
    grads = both[:, CAP:].reshape(n * CAP, -1).astype(BF16)
    before = nn(rows, w_in[0])
    scale = np.float32(np.sqrt(2 / np.pi))
    inner = jnp.tanh(scale * (before + 0.044715 * before * before * before))
    acted = (0.5 * before * (1.0 + inner)).astype(BF16)
    slope = 0.5 * (1.0 + inner) + 0.5 * before * (1.0 - inner * inner) * scale * (
        1.0 + 3 * 0.044715 * before * before
    )
    result = nn(acted, w_out[0])
    grad_before = (slope * nt(grads, w_out[0])).astype(BF16)
    back = nt(grad_before, w_in[0])
    part[...] = jnp.concatenate(
        [result.reshape(n, CAP, -1), back.reshape(n, CAP, -1)], axis=1
    ).astype(BF16)
    grad_in[0] = tn(rows, grad_before)
    grad_out[0] = tn(acted, grads)


def backward_kernel(
    length, tok, attn, gain_two, router, route_row, route_col, cot, back, hid, qkv, heads, w, rel, picks,
    result, grad_mixed, gw, gh, small, table, gproj,
):
    mixed, inv, unit, hidden, probs, hot_col, gate, match = middle(
        length[0], tok, attn, gain_two, router, route_row, route_col
    )
    n = back.shape[0]
    size = tok.shape[0]
    both = back[...].astype(F32)
    out_rows = both[:, :CAP].reshape(n * CAP, -1).astype(BF16)
    back_rows = both[:, CAP:].reshape(n * CAP, -1).astype(BF16)
    expert_result = tn(match, out_rows)
    upstream = cot[...].astype(F32)
    result[...] = (mixed + gate * expert_result).astype(BF16)
    grad_gate = jnp.sum(upstream * expert_result, axis=-1, keepdims=True)
    grad_logits = probs * (jnp.where(hot_col, grad_gate, 0.0) - gate * grad_gate)
    grad_low = grad_logits.astype(BF16)
    grad_rest = (grad_logits - grad_low.astype(F32)).astype(BF16)
    small[0 : router.shape[0]] = tn(grad_low, hidden) + tn(grad_rest, hidden)
    grad_hidden = tn(match, back_rows) + nn(grad_low, router[...]) + nn(grad_rest, router[...])
    small[router.shape[0] : router.shape[0] + 1] = jnp.sum(grad_hidden * unit, axis=0, keepdims=True)
    scaled = grad_hidden * gain_two[...]
    gm = upstream + inv * (scaled - unit * jnp.mean(scaled * unit, axis=-1, keepdims=True))
    grad_mixed[...] = gm
    gattn = gm.astype(BF16)
    gw[3] = tn(gattn, heads[...]).astype(BF16)
    grad_heads = nn(gattn, w[3]).astype(BF16)
    flip = jnp.where(
        lax.broadcasted_iota(jnp.int32, (size, size), 0)
        + lax.broadcasted_iota(jnp.int32, (size, size), 1)
        == size - 1,
        1.0,
        0.0,
    ).astype(BF16)
    for h in range(qkv.shape[2] // DH):
        at = slice(h * DH, (h + 1) * DH)
        q, k, v = qkv[0, :, at], qkv[1, :, at], qkv[2, :, at]
        probs_full = head_scores(q, k, rel[h : h + 1], length[0], h)
        gheads = grad_heads[:, at]
        gprobs = nt(gheads, v)
        dot = jnp.sum(probs_full * gprobs, axis=-1, keepdims=True)
        gscores = (probs_full * (gprobs - dot)).astype(BF16)
        gproj[2, :, at] = tn(probs_full.astype(BF16), gheads).astype(BF16)
        gproj[0, :, at] = (nn(gscores, k) * DH ** (-0.5)).astype(BF16)
        gproj[1, :, at] = (tn(gscores, q) * DH ** (-0.5)).astype(BF16)
        turned = nn(flip, gscores)
        turned = jnp.concatenate([turned, jnp.zeros((size, size), F32)], axis=1)
        turned = pltpu.roll(turned, 0, 1, stride=1, stride_axis=0)
        diagonal = jnp.sum(turned, axis=0, keepdims=True)
        table[h : h + 1] = nn(diagonal, picks[...], highest)
    ghid = jnp.zeros(tok.shape, F32)
    for m in range(3):
        gw[m] = tn(hid[...], gproj[m]).astype(BF16)
        ghid = ghid + nt(gproj[m], w[m])
    gh[...] = ghid.astype(BF16)
    rows_in = tok[...].astype(F32)
    unit_one = rows_in * lax.rsqrt(jnp.mean(rows_in * rows_in, axis=-1, keepdims=True) + epsilon)
    small[router.shape[0] + 1 : router.shape[0] + 2] = jnp.sum(ghid * unit_one, axis=0, keepdims=True)


def bucket_picks(length, buckets):
    offset = np.arange(2 * length) - (length - 1)
    distance = np.abs(offset)
    beyond = np.sum(distance[:, None] >= thresholds, axis=-1)
    bucket = (offset > 0) * 16 + np.minimum(distance, 8) + beyond
    return (bucket[:, None] == np.arange(buckets)[None, :]).astype(np.float32)


def body(
    n_exp, n_col, n_row,
    tokens, qkv_weight, out_weight, bias_table, gain_attn, gain_expert, router_weight,
    expert_in, expert_out, lengths, routes, cotangent,
):
    n = n_exp * n_col
    size, width = tokens.shape
    shard = width // n
    local = qkv_weight.shape[2]
    heads_local = local // DH
    experts = router_weight.shape[1]
    lines = -(-(experts + 2) // 16) * 16
    dma = lambda k: pltpu.SemaphoreType.DMA((k,))
    packed = jnp.concatenate([qkv_weight, out_weight.T[None]], axis=0)
    small = jnp.concatenate(
        [router_weight.T, gain_attn[None], gain_expert[None]], axis=0
    )
    small = jnp.pad(small, ((0, lines - experts - 2), (0, 128 - shard)))
    w_all, s_all = call(
        functools.partial(gather_kernel, n_exp),
        [((n_exp, n_col) + packed.shape, BF16), ((n_exp, n_col) + small.shape, BF16)],
        [packed, small],
        [dma(n_exp - 1)] * 4 + [dma(n_exp)] * 4,
        1,
    )
    w = w_all.reshape(n, 4, shard, local).transpose(1, 0, 2, 3).reshape(4, width, local)
    s = s_all.reshape(n, lines, 128)[:, :, :shard].transpose(1, 0, 2).reshape(lines, width)
    router = s[:experts]
    gain_one = s[experts : experts + 1].astype(F32)
    gain_two = s[experts + 1 : experts + 2].astype(F32)
    picks = bucket_picks(size, bias_table.shape[0])
    rel = jnp.dot(
        bias_table.T, jnp.asarray(picks.T, BF16), preferred_element_type=F32
    )
    route_row = routes.reshape(1, size)
    hid, qkv, heads, attn_part = call(
        forward_kernel,
        [((size, width), BF16), ((3, size, local), BF16), ((size, local), BF16), ((size, width), BF16)],
        [lengths, tokens, w, gain_one, rel],
        specs=[SMEM] + [VMEM] * 4,
    )
    block = size // n_row
    (attn,) = call(
        functools.partial(row_sum_kernel, n_row),
        [((n_row, block, width), BF16)],
        [attn_part.reshape(n_row, block, width)],
        [pltpu.VMEM((n_row - 1, block, width), BF16)] + [dma(n_row - 1)] * 4,
        2,
    )
    attn = attn.reshape(size, width)
    (sent,) = call(
        send_kernel,
        [((n, 2 * CAP, width), BF16)],
        [lengths, tokens, attn, gain_two, router, route_row, routes, cotangent],
        specs=[SMEM] + [VMEM] * 7,
    )
    (arrived,) = call(
        functools.partial(dispatch_kernel, n_exp, n_col),
        [((n, 2 * CAP, width), BF16)],
        [sent],
        [dma(n - 1)] * 2,
        3,
    )
    part, grad_expert_in, grad_expert_out = call(
        expert_kernel,
        [((n, 2 * CAP, width), BF16), (expert_in.shape, F32), (expert_out.shape, F32)],
        [arrived, expert_in, expert_out],
    )
    share = n // n_row
    (back,) = call(
        functools.partial(return_kernel, n_exp, n_col, n_row),
        [((n, 2 * CAP, width), BF16)],
        [part],
        [
            pltpu.VMEM((n_row - 1, share, 2 * CAP, width), BF16),
            pltpu.VMEM((share, 2 * CAP, width), BF16),
            dma(n_row - 1),
            dma(n_row - 1),
            dma(share * n_row),
            dma(n),
        ],
        4,
    )
    result, grad_mixed, gw, gh, grads, table = call(
        backward_kernel,
        [
            ((size, width), BF16),
            ((size, width), F32),
            ((4, width, local), BF16),
            ((size, width), BF16),
            ((lines, width), F32),
            ((heads_local, bias_table.shape[0]), F32),
        ],
        [
            lengths, tokens, attn, gain_two, router, route_row, routes, cotangent, back,
            hid, qkv, heads, w, rel, jnp.asarray(picks),
        ],
        [pltpu.VMEM((3, size, local), BF16)],
        specs=[SMEM] + [VMEM] * 14,
    )
    gw = gw.reshape(4, n_exp, n_col, shard, local).transpose(2, 1, 0, 3, 4)
    lead = jnp.concatenate(
        [grads[:8], grads[experts : experts + 2], grads[8:experts]], axis=0
    )
    lead = lead.reshape(experts + 2, n, shard).transpose(1, 0, 2)
    lead = jnp.pad(lead, ((0, 0), (0, lines - experts - 2), (0, 128 - shard)))
    tail = jnp.pad(table, ((0, 8 - heads_local), (0, 128 - table.shape[1])))
    lead = jnp.concatenate([lead, jnp.broadcast_to(tail[None], (n, 8, 128))], axis=1)
    high = lines + 8
    gt, gwo, smo = call(
        functools.partial(final_kernel, n_exp, n_col, n_row),
        [((n_row, block, width), BF16), ((4, shard, local), F32), ((high, 128), F32)],
        [
            gw, lead, gh.reshape(n_row, block, width), tokens.reshape(n_row, block, width),
            grad_mixed.reshape(n_row, block, width), gain_one,
        ],
        [
            pltpu.VMEM((n_row - 1, block, width), BF16),
            pltpu.VMEM((n_exp, 4, shard, local), BF16),
            pltpu.VMEM((n_exp, 4, shard, local), BF16),
            pltpu.VMEM((n_exp - 1, 4, shard, local), BF16),
            pltpu.VMEM((n - 1, high, 128), F32),
            pltpu.VMEM((n_row, high, 128), F32),
            dma(n_row - 1), dma(n_row - 1), dma(n_row - 1), dma(n_row - 1),
            pltpu.SemaphoreType.DMA, pltpu.SemaphoreType.DMA,
            dma(n_exp - 1), dma(n_exp - 1),
            dma(n - 1), dma(n - 1), dma(n_row - 1), dma(n_row - 1),
        ],
        5,
    )
    grad_router = jnp.concatenate([smo[:8], smo[10 : experts + 2]], axis=0)[:, :shard].T
    return (
        result,
        gt.reshape(size, width),
        gwo[:3],
        gwo[3].T,
        smo[lines : lines + heads_local, : bias_table.shape[0]].T,
        smo[9, :shard],
        smo[8, :shard],
        grad_router,
        grad_expert_in,
        grad_expert_out,
    )


def solution(mesh):
    both = ("exp", "col")
    placed = (
        P(both, None),
        P(None, both, "row"),
        P("row", both),
        P(None, "row"),
        P(both),
        P(both),
        P(both, None),
        P(both, None, "row"),
        P(both, "row", None),
        P(both),
        P(both, None),
        P(both, None),
    )
    shape = mesh.shape
    return jax.shard_map(
        functools.partial(body, shape["exp"], shape["col"], shape["row"]),
        mesh=mesh,
        in_specs=placed,
        out_specs=(
            P(both, None),
            P(both, None),
            P(None, both, "row"),
            P("row", both),
            P(None, "row"),
            P(both),
            P(both),
            P(both, None),
            P(both, None, "row"),
            P(both, "row", None),
        ),
        check_vma=False,
    )
```

```python
import functools

import jax
import jax.numpy as jnp
import numpy as np
from jax import lax
from jax.experimental import pallas as pl
from jax.experimental.pallas import tpu as pltpu
from jax.sharding import PartitionSpec as P

DH = 64
CAP = 8
F32 = jnp.float32
BF16 = jnp.bfloat16
epsilon = 1e-06
thresholds = np.array([12, 16, 23, 32, 46, 64, 91], dtype=np.int32)
highest = lax.Precision.HIGHEST
MESH = pl.DeviceIdType.MESH
LIMIT = 56 * 1024 * 1024
VMEM = pl.BlockSpec(memory_space=pltpu.VMEM)
SMEM = pl.BlockSpec(memory_space=pltpu.SMEM)


def nt(a, b, precision=None):
    return lax.dot_general(
        a, b, (((1,), (1,)), ((), ())), preferred_element_type=F32, precision=precision
    )


def tn(a, b, precision=None):
    return lax.dot_general(
        a, b, (((0,), (0,)), ((), ())), preferred_element_type=F32, precision=precision
    )


def nn(a, b, precision=None):
    return jnp.dot(a, b, preferred_element_type=F32, precision=precision)


def call(kernel, outs, args, scratch=(), collective=None, specs=None):
    params = dict(vmem_limit_bytes=LIMIT)
    if collective is not None:
        params.update(collective_id=collective, has_side_effects=True)
    return pl.pallas_call(
        kernel,
        out_shape=[jax.ShapeDtypeStruct(s, d) for s, d in outs],
        in_specs=specs or [VMEM] * len(args),
        out_specs=[VMEM] * len(outs),
        scratch_shapes=list(scratch),
        compiler_params=pltpu.CompilerParams(**params),
    )(*args)


def greet(peers):
    barrier = pltpu.get_barrier_semaphore()
    for peer in peers:
        pl.semaphore_signal(barrier, inc=1, device_id=peer, device_id_type=MESH)


def meet(peers):
    pl.semaphore_wait(pltpu.get_barrier_semaphore(), len(peers))


def enter(peers):
    greet(peers)
    meet(peers)


def remote(src, dst, send, recv, peer):
    copy = pltpu.make_async_remote_copy(
        src_ref=src, dst_ref=dst, send_sem=send, recv_sem=recv, device_id=peer, device_id_type=MESH
    )
    copy.start()
    return copy


def ring(axis, size):
    me = lax.axis_index(axis)
    return [lax.rem(me + k, size) for k in range(1, size)]


def group_peers(n_exp, n_col):
    n = n_exp * n_col
    me = lax.axis_index("exp") * n_col + lax.axis_index("col")
    return [lax.rem(me + k, n) for k in range(1, n)]


def gather_kernel(n_exp, w, s, w_all, s_all, send, recv, send_s, recv_s, c_send, c_recv, d_send, d_recv):
    e = lax.axis_index("exp")
    c = lax.axis_index("col")
    other = {"col": 1 - c}
    peers = ring("exp", n_exp)
    enter([{"exp": p} for p in peers] + [other])
    copies = []
    for k, p in enumerate(peers):
        copies.append(remote(s, s_all.at[e, c], send_s.at[k], recv_s.at[k], {"exp": p}))
        copies.append(remote(w, w_all.at[e, c], send.at[k], recv.at[k], {"exp": p}))
    last = [
        remote(s, s_all.at[e, c], d_send.at[0], d_recv.at[0], other),
        remote(w, w_all.at[e, c], c_send.at[0], c_recv.at[0], other),
    ]
    w_all[e, c] = w[...]
    s_all[e, c] = s[...]
    for k in range(n_exp - 1):
        q = lax.rem(e + n_exp - k - 1, n_exp)
        copies[2 * k].wait_recv()
        last.append(remote(s_all.at[q, c], s_all.at[q, c], d_send.at[k + 1], d_recv.at[k + 1], other))
        copies[2 * k + 1].wait_recv()
        last.append(remote(w_all.at[q, c], w_all.at[q, c], c_send.at[k + 1], c_recv.at[k + 1], other))
    for copy in copies:
        copy.wait_send()
    for copy in last:
        copy.wait()


def bias_grid(rel_row, size):
    x = jnp.broadcast_to(rel_row, (size, 2 * size))
    return pltpu.roll(x, size + 1, 1, stride=1, stride_axis=0)[:, :size]


def head_probs(q, k, bias, length):
    scores = nt(q, k) * DH ** (-0.5) + bias
    key_at = lax.broadcasted_iota(jnp.int32, (1, k.shape[0]), 1)
    scores = jnp.where(key_at < length, scores, -1e30)
    top = jnp.max(scores, axis=-1, keepdims=True)
    raised = jnp.exp(scores - top)
    return raised * (1.0 / jnp.sum(raised, axis=-1, keepdims=True))


def forward_kernel(
    n_row, length, tok, w_in, gain, rel,
    w, hid, qkv, heads, out,
    bias, x, held, send, recv, send2, recv2,
):
    r = lax.axis_index("row")
    peers = ring("row", n_row)
    ids = [{"row": p} for p in peers]
    greet(ids)
    size = tok.shape[0]
    block = size // n_row
    local = qkv.shape[2]
    if len(w_in.shape) == 3:
        w[...] = w_in[...]
    else:
        _, n_col, _, shard, _ = w_in.shape
        for e in range(w_in.shape[0]):
            for c in range(n_col):
                at = (e * n_col + c) * shard
                w[:, at : at + shard] = w_in[e, c]
    rows_in = tok[...].astype(F32)
    inv = lax.rsqrt(jnp.mean(rows_in * rows_in, axis=-1, keepdims=True) + epsilon)
    hid[...] = (rows_in * inv * gain[...]).astype(BF16)
    for m in range(3):
        qkv[m] = nn(hid[...], w[m]).astype(BF16)
    for h in range(local // DH):
        bias[h] = bias_grid(rel[h : h + 1], size)
    copies = []
    for k, p in enumerate(peers + [r]):
        rows = pl.ds(pl.multiple_of(p * block, block), block)
        for h in range(local // DH):
            at = slice(h * DH, (h + 1) * DH)
            probs = head_probs(qkv[0, rows, at], qkv[1, :, at], bias[h, rows], length[0])
            heads[rows, at] = nn(probs.astype(BF16), qkv[2, :, at]).astype(BF16)
        x[k] = nt(heads[rows, :], w[3]).astype(BF16)
        if k == 0:
            meet(ids)
        if k < n_row - 1:
            copies.append(remote(x.at[k], held.at[k], send.at[k], recv.at[k], {"row": p}))
    total = x[n_row - 1].astype(F32)
    for k, copy in enumerate(copies):
        copy.wait_recv()
        total = total + held[k].astype(F32)
    out[r] = total.astype(BF16)
    more = [
        remote(out.at[r], out.at[r], send2.at[k], recv2.at[k], {"row": p})
        for k, p in enumerate(peers)
    ]
    for copy in copies:
        copy.wait_send()
    for copy in more:
        copy.wait()


def middle(length, tok, attn, gain, router, route_row, route_col):
    size = tok.shape[0]
    experts = router.shape[0]
    mixed = tok[...].astype(F32) + attn[...].astype(F32)
    inv = lax.rsqrt(jnp.mean(mixed * mixed, axis=-1, keepdims=True) + epsilon)
    unit = mixed * inv
    hidden = (unit * gain[...]).astype(BF16)
    logits = nt(hidden, router[...])
    top = jnp.max(logits, axis=-1, keepdims=True)
    raised = jnp.exp(logits - top)
    probs = raised / jnp.sum(raised, axis=-1, keepdims=True)
    hot_col = lax.broadcasted_iota(jnp.int32, (size, experts), 1) == route_col[...]
    gate = jnp.sum(jnp.where(hot_col, probs, 0.0), axis=-1, keepdims=True)
    live = lax.broadcasted_iota(jnp.int32, (1, size), 1) < length
    hot = (lax.broadcasted_iota(jnp.int32, (experts, size), 0) == route_row[...]) & live
    hot = jnp.where(hot, 1.0, 0.0)
    earlier = jnp.where(
        lax.broadcasted_iota(jnp.int32, (size, size), 0)
        < lax.broadcasted_iota(jnp.int32, (size, size), 1),
        1.0,
        0.0,
    )
    before = nn(hot.astype(BF16), earlier.astype(BF16))
    rank = jnp.sum(hot * before, axis=0, keepdims=True).astype(jnp.int32)
    kept = live & (rank < CAP)
    target = jnp.where(kept, route_row[...] * CAP + rank, -1)
    match = lax.broadcasted_iota(jnp.int32, (experts * CAP, size), 0) == target
    match = jnp.where(match, 1.0, 0.0).astype(BF16)
    return mixed, inv, unit, hidden, probs, hot_col, gate, match


def expert_kernel(
    n_exp, n_col, n_row,
    length, tok, attn, gain, router, route_row, route_col, cot, w_in, w_out,
    out, rows, grads, acted, grad_before,
    sent, arrived, part, held, total, send0, recv0, send, recv, send2, recv2,
):
    n = n_exp * n_col
    share = n // n_row
    r = lax.axis_index("row")
    me = lax.axis_index("exp") * n_col + lax.axis_index("col")
    mine = me // share == r
    everyone = [
        (lax.rem(r + b, n_row), lax.rem(me + k, n))
        for b in range(n_row)
        for k in range(n)
        if b or k
    ]
    everyone = [{"exp": k // n_col, "col": lax.rem(k, n_col), "row": b} for b, k in everyone]
    greet(everyone)
    _, _, _, hidden, _, _, gate, match = middle(
        length[0], tok, attn, gain, router, route_row, route_col
    )
    grad = (gate * cot[...].astype(F32)).astype(BF16)
    first = nn(match, hidden).reshape(n, CAP, -1)
    second = nn(match, grad).reshape(n, CAP, -1)
    sent[...] = jnp.concatenate([first, second], axis=1).astype(BF16)
    meet(everyone)
    group = group_peers(n_exp, n_col)
    copies = [
        remote(
            sent.at[p],
            arrived.at[me],
            send0.at[k],
            recv0.at[k],
            {"exp": p // n_col, "col": lax.rem(p, n_col)},
        )
        for k, p in enumerate(group)
    ]
    arrived[me] = sent[me]
    for copy in copies:
        copy.wait()
    both = arrived[...].astype(F32)
    rows[...] = both[:, :CAP].reshape(n * CAP, -1).astype(BF16)
    grads[...] = both[:, CAP:].reshape(n * CAP, -1).astype(BF16)
    before = nn(rows[...], w_in[0])
    scale = np.float32(np.sqrt(2 / np.pi))
    inner = jnp.tanh(scale * (before + 0.044715 * before * before * before))
    acted[...] = (0.5 * before * (1.0 + inner)).astype(BF16)
    slope = 0.5 * (1.0 + inner) + 0.5 * before * (1.0 - inner * inner) * scale * (
        1.0 + 3 * 0.044715 * before * before
    )
    result = nn(acted[...], w_out[0])
    grad_before[...] = (slope * nt(grads[...], w_out[0])).astype(BF16)
    back = nt(grad_before[...], w_in[0])
    part[...] = jnp.concatenate(
        [result.reshape(n, CAP, -1), back.reshape(n, CAP, -1)], axis=1
    ).astype(BF16)
    copies = [
        remote(part.at[pl.ds(p * share, share)], held.at[k], send.at[k], recv.at[k], {"row": p})
        for k, p in enumerate(ring("row", n_row))
    ]
    acc = part[pl.ds(r * share, share)].astype(F32)
    for k, copy in enumerate(copies):
        copy.wait_recv()
        acc = acc + held[k].astype(F32)
    total[...] = acc.astype(BF16)
    started = []
    for g in range(share):
        for b in range(n_row):
            t = r * share + g
            own = mine & (t == me) & (r == b)
            copy = pltpu.make_async_remote_copy(
                src_ref=total.at[g],
                dst_ref=out.at[me],
                send_sem=send2.at[g * n_row + b],
                recv_sem=recv2.at[me],
                device_id={"exp": t // n_col, "col": lax.rem(t, n_col), "row": b},
                device_id_type=MESH,
            )

            @pl.when(own)
            def _(g=g):
                out[me] = total[g]

            @pl.when(jnp.logical_not(own))
            def _(copy=copy):
                copy.start()

            started.append((own, copy))

    for own, copy in started:

        @pl.when(jnp.logical_not(own))
        def _(copy=copy):
            copy.wait_send()

    for copy in copies:
        copy.wait_send()
    for k in range(n):

        @pl.when(jnp.logical_not((k == me) & mine))
        def _(k=k):
            pltpu.make_async_remote_copy(
                src_ref=total.at[0],
                dst_ref=out.at[k],
                send_sem=send2.at[0],
                recv_sem=recv2.at[k],
                device_id={"row": r},
                device_id_type=MESH,
            ).wait_recv()


def expert_grad_kernel(rows, grads, acted, grad_before, grad_in, grad_out):
    grad_in[0] = tn(rows[...], grad_before[...])
    grad_out[0] = tn(acted[...], grads[...])


def backward_kernel(
    n_exp, n_col, n_row,
    length, tok, attn, gain_one, gain_two, router, route_row, route_col, cot, back, hid, qkv, heads,
    w, rel, picks,
    result, gt, gwo, smo,
    gproj, gw, gm, gh, sm, hrow, sib, pre, zheld, smheld, smrow,
    s_row, r_row, s_row2, r_row2, s_sib, r_sib, s_z, r_z, s_sm, r_sm, s_sm2, r_sm2,
):
    e = lax.axis_index("exp")
    c = lax.axis_index("col")
    r = lax.axis_index("row")
    n = n_exp * n_col
    me = e * n_col + c
    rows = ring("row", n_row)
    exps = ring("exp", n_exp)
    group = group_peers(n_exp, n_col)
    ids = [{"exp": p // n_col, "col": lax.rem(p, n_col)} for p in group]
    everyone = [{"row": p} for p in rows] + ids
    greet(everyone)
    size, width = tok.shape
    block = size // n_row
    shard = width // n
    experts = router.shape[0]
    local = qkv.shape[2]

    def place(m, grad):
        for k in range(n):
            gw[k % n_col, k // n_col, m] = grad[k * shard : (k + 1) * shard].astype(BF16)

    mixed, inv, unit, hidden, probs, hot_col, gate, match = middle(
        length[0], tok, attn, gain_two, router, route_row, route_col
    )
    both = back[...].astype(F32)
    out_rows = both[:, :CAP].reshape(n * CAP, -1).astype(BF16)
    back_rows = both[:, CAP:].reshape(n * CAP, -1).astype(BF16)
    expert_result = tn(match, out_rows)
    upstream = cot[...].astype(F32)
    result[...] = (mixed + gate * expert_result).astype(BF16)
    grad_gate = jnp.sum(upstream * expert_result, axis=-1, keepdims=True)
    grad_logits = probs * (jnp.where(hot_col, grad_gate, 0.0) - gate * grad_gate)
    grad_low = grad_logits.astype(BF16)
    grad_rest = (grad_logits - grad_low.astype(F32)).astype(BF16)
    grad_router = tn(grad_low, hidden) + tn(grad_rest, hidden)
    grad_hidden = tn(match, back_rows) + nn(grad_low, router[...]) + nn(grad_rest, router[...])
    grad_gain_two = jnp.sum(grad_hidden * unit, axis=0, keepdims=True)
    scaled = grad_hidden * gain_two[...]
    gm[...] = upstream + inv * (scaled - unit * jnp.mean(scaled * unit, axis=-1, keepdims=True))
    gattn = gm[...].astype(BF16)
    place(3, tn(gattn, heads[...]))
    grad_heads = nn(gattn, w[3]).astype(BF16)
    flip = jnp.where(
        lax.broadcasted_iota(jnp.int32, (size, size), 0)
        + lax.broadcasted_iota(jnp.int32, (size, size), 1)
        == size - 1,
        1.0,
        0.0,
    ).astype(BF16)
    sm[...] = jnp.zeros(sm.shape, F32)
    lines = experts + 2
    for h in range(local // DH):
        at = slice(h * DH, (h + 1) * DH)
        q, k, v = qkv[0, :, at], qkv[1, :, at], qkv[2, :, at]
        probs_full = head_probs(q, k, bias_grid(rel[h : h + 1], size), length[0])
        gheads = grad_heads[:, at]
        gprobs = nt(gheads, v)
        dot = jnp.sum(probs_full * gprobs, axis=-1, keepdims=True)
        gscores = (probs_full * (gprobs - dot)).astype(BF16)
        gproj[2, :, at] = tn(probs_full.astype(BF16), gheads).astype(BF16)
        gproj[0, :, at] = (nn(gscores, k) * DH ** (-0.5)).astype(BF16)
        gproj[1, :, at] = (tn(gscores, q) * DH ** (-0.5)).astype(BF16)
        turned = nn(flip, gscores)
        turned = jnp.concatenate([turned, jnp.zeros((size, size), F32)], axis=1)
        turned = pltpu.roll(turned, 0, 1, stride=1, stride_axis=0)
        diagonal = jnp.sum(turned, axis=0, keepdims=True)
        line = nn(diagonal, picks[...], highest)
        for k in range(n):
            sm[k, lines + h : lines + h + 1, 0 : line.shape[1]] = line
    row_copies = []
    grad_gain_one = jnp.zeros((1, width), F32)
    for k, p in enumerate(rows + [r]):
        at = pl.ds(pl.multiple_of(p * block, block), block)
        ghid = nt(gproj[0, at, :], w[0]) + nt(gproj[1, at, :], w[1]) + nt(gproj[2, at, :], w[2])
        rows_in = tok[at, :].astype(F32)
        inv_one = lax.rsqrt(jnp.mean(rows_in * rows_in, axis=-1, keepdims=True) + epsilon)
        unit_one = rows_in * inv_one
        grad_gain_one = grad_gain_one + jnp.sum(ghid * unit_one, axis=0, keepdims=True)
        if k == 0:
            meet(everyone)
        if k < n_row - 1:
            gh[k] = ghid.astype(BF16)
            row_copies.append(remote(gh.at[k], hrow.at[k], s_row.at[k], r_row.at[k], {"row": p}))
    for m in range(3):
        place(m, tn(hid[...], gproj[m]))
    sibling = remote(gw.at[1 - c], sib, s_sib, r_sib, {"col": 1 - c})
    for k in range(n):
        at = slice(k * shard, (k + 1) * shard)
        sm[k, 0:experts, 0:shard] = grad_router[:, at]
        sm[k, experts : experts + 1, 0:shard] = grad_gain_two[:, at]
        sm[k, experts + 1 : experts + 2, 0:shard] = grad_gain_one[:, at]
    small = [
        remote(sm.at[p], smheld.at[k], s_sm.at[k], r_sm.at[k], ids[k]) for k, p in enumerate(group)
    ]
    sibling.wait_recv()
    pre[...] = (gw[c].astype(F32) + sib[...].astype(F32)).astype(BF16)
    z_copies = [
        remote(pre.at[p], zheld.at[k], s_z.at[k], r_z.at[k], {"exp": p}) for k, p in enumerate(exps)
    ]
    total = ghid
    for k, copy in enumerate(row_copies):
        copy.wait_recv()
        total = total + hrow[k].astype(F32)
    scaled = total * gain_one[...]
    own = pl.ds(pl.multiple_of(r * block, block), block)
    gt[r] = (
        gm[own, :]
        + inv_one * (scaled - unit_one * jnp.mean(scaled * unit_one, axis=-1, keepdims=True))
    ).astype(BF16)
    row_copies2 = [
        remote(gt.at[r], gt.at[r], s_row2.at[k], r_row2.at[k], {"row": p}) for k, p in enumerate(rows)
    ]
    part = sm[me]
    for k, copy in enumerate(small):
        copy.wait_recv()
        part = part + smheld[k]
    smrow[0] = part
    small2 = [
        remote(smrow.at[0], smrow.at[k + 1], s_sm2.at[k], r_sm2.at[k], {"row": p})
        for k, p in enumerate(rows)
    ]
    full = part
    for k, copy in enumerate(small2):
        copy.wait_recv()
        full = full + smrow[k + 1]
    row_at = lax.broadcasted_iota(jnp.int32, part.shape, 0)
    smo[...] = jnp.where(row_at == experts + 1, full, part)
    wsum = pre[e].astype(F32)
    for k, copy in enumerate(z_copies):
        copy.wait_recv()
        wsum = wsum + zheld[k].astype(F32)
    gwo[...] = wsum
    for copy in [sibling] + row_copies + small + z_copies + small2:
        copy.wait_send()
    for copy in row_copies2:
        copy.wait()


def bucket_picks(length, buckets):
    offset = np.arange(2 * length) - (length - 1)
    distance = np.abs(offset)
    beyond = np.sum(distance[:, None] >= thresholds, axis=-1)
    bucket = (offset > 0) * 16 + np.minimum(distance, 8) + beyond
    return (bucket[:, None] == np.arange(buckets)[None, :]).astype(np.float32)


def body(
    n_exp, n_col, n_row,
    tokens, qkv_weight, out_weight, bias_table, gain_attn, gain_expert, router_weight,
    expert_in, expert_out, lengths, routes, cotangent,
):
    n = n_exp * n_col
    size, width = tokens.shape
    shard = width // n
    local = qkv_weight.shape[2]
    heads_local = local // DH
    experts = router_weight.shape[1]
    lines = -(-(experts + 2) // 16) * 16
    dma = lambda k: pltpu.SemaphoreType.DMA((k,))
    packed = jnp.concatenate([qkv_weight, out_weight.T[None]], axis=0)
    small = jnp.concatenate(
        [router_weight.T, gain_attn[None], gain_expert[None]], axis=0
    )
    small = jnp.pad(small, ((0, lines - experts - 2), (0, 128 - shard)))
    w_all, s_all = call(
        functools.partial(gather_kernel, n_exp),
        [((n_exp, n_col) + packed.shape, BF16), ((n_exp, n_col) + small.shape, BF16)],
        [packed, small],
        [dma(n_exp - 1)] * 4 + [dma(n_exp)] * 4,
        1,
    )
    if shard % 16:
        w_all = w_all.reshape(n, 4, shard, local).transpose(1, 0, 2, 3).reshape(4, width, local)
    s = s_all.reshape(n, lines, 128)[:, :, :shard].transpose(1, 0, 2).reshape(lines, width)
    router = s[:experts]
    gain_one = s[experts : experts + 1].astype(F32)
    gain_two = s[experts + 1 : experts + 2].astype(F32)
    picks = bucket_picks(size, bias_table.shape[0])
    rel = jnp.dot(
        bias_table.T, jnp.asarray(picks.T, BF16), preferred_element_type=F32
    )
    route_row = routes.reshape(1, size)
    block = size // n_row
    w, hid, qkv, heads, attn = call(
        functools.partial(forward_kernel, n_row),
        [
            ((4, width, local), BF16),
            ((size, width), BF16),
            ((3, size, local), BF16),
            ((size, local), BF16),
            ((n_row, block, width), BF16),
        ],
        [lengths, tokens, w_all, gain_one, rel],
        [
            pltpu.VMEM((heads_local, size, size), F32),
            pltpu.VMEM((n_row, block, width), BF16),
            pltpu.VMEM((n_row - 1, block, width), BF16),
        ]
        + [dma(n_row - 1)] * 4,
        2,
        specs=[SMEM] + [VMEM] * 4,
    )
    attn = attn.reshape(size, width)
    share = n // n_row
    slots = pltpu.VMEM((n, 2 * CAP, width), BF16)
    back, *saved = call(
        functools.partial(expert_kernel, n_exp, n_col, n_row),
        [
            ((n, 2 * CAP, width), BF16),
            ((n * CAP, width), BF16),
            ((n * CAP, width), BF16),
            ((n * CAP, expert_in.shape[2]), BF16),
            ((n * CAP, expert_in.shape[2]), BF16),
        ],
        [
            lengths, tokens, attn, gain_two, router, route_row, routes, cotangent, expert_in,
            expert_out,
        ],
        [
            slots, slots, slots,
            pltpu.VMEM((n_row - 1, share, 2 * CAP, width), BF16),
            pltpu.VMEM((share, 2 * CAP, width), BF16),
            dma(n - 1), dma(n - 1), dma(n_row - 1), dma(n_row - 1), dma(share * n_row), dma(n),
        ],
        3,
        specs=[SMEM] + [VMEM] * 9,
    )
    grad_expert_in, grad_expert_out = call(
        expert_grad_kernel, [(expert_in.shape, F32), (expert_out.shape, F32)], saved
    )
    high = -(-(experts + 2 + heads_local) // 8) * 8
    result, gt, gwo, smo = call(
        functools.partial(backward_kernel, n_exp, n_col, n_row),
        [
            ((size, width), BF16),
            ((n_row, block, width), BF16),
            ((4, shard, local), F32),
            ((high, 128), F32),
        ],
        [
            lengths, tokens, attn, gain_one, gain_two, router, route_row, routes, cotangent, back,
            hid, qkv, heads, w, rel, jnp.asarray(picks),
        ],
        [
            pltpu.VMEM((3, size, local), BF16),
            pltpu.VMEM((n_col, n_exp, 4, shard, local), BF16),
            pltpu.VMEM((size, width), F32),
            pltpu.VMEM((n_row - 1, block, width), BF16),
            pltpu.VMEM((n, high, 128), F32),
            pltpu.VMEM((n_row - 1, block, width), BF16),
            pltpu.VMEM((n_exp, 4, shard, local), BF16),
            pltpu.VMEM((n_exp, 4, shard, local), BF16),
            pltpu.VMEM((n_exp - 1, 4, shard, local), BF16),
            pltpu.VMEM((n - 1, high, 128), F32),
            pltpu.VMEM((n_row, high, 128), F32),
            dma(n_row - 1), dma(n_row - 1), dma(n_row - 1), dma(n_row - 1),
            pltpu.SemaphoreType.DMA, pltpu.SemaphoreType.DMA,
            dma(n_exp - 1), dma(n_exp - 1),
            dma(n - 1), dma(n - 1), dma(n_row - 1), dma(n_row - 1),
        ],
        4,
        specs=[SMEM] + [VMEM] * 15,
    )
    lines = experts + 2
    return (
        result,
        gt.reshape(size, width),
        gwo[:3],
        gwo[3].T,
        smo[lines : lines + heads_local, : bias_table.shape[0]].T,
        smo[experts + 1, :shard],
        smo[experts, :shard],
        smo[:experts, :shard].T,
        grad_expert_in,
        grad_expert_out,
    )


def solution(mesh):
    both = ("exp", "col")
    placed = (
        P(both, None),
        P(None, both, "row"),
        P("row", both),
        P(None, "row"),
        P(both),
        P(both),
        P(both, None),
        P(both, None, "row"),
        P(both, "row", None),
        P(both),
        P(both, None),
        P(both, None),
    )
    shape = mesh.shape
    return jax.shard_map(
        functools.partial(body, shape["exp"], shape["col"], shape["row"]),
        mesh=mesh,
        in_specs=placed,
        out_specs=(
            P(both, None),
            P(both, None),
            P(None, both, "row"),
            P("row", both),
            P(None, "row"),
            P(both),
            P(both),
            P(both, None),
            P(both, None, "row"),
            P(both, "row", None),
        ),
        check_vma=False,
    )
```

```python
import functools

import jax
import jax.numpy as jnp
import numpy as np
from jax import lax
from jax.experimental import pallas as pl
from jax.experimental.pallas import tpu as pltpu
from jax.sharding import PartitionSpec as P

DH = 64
CAP = 8
F32 = jnp.float32
BF16 = jnp.bfloat16
epsilon = 1e-06
thresholds = np.array([12, 16, 23, 32, 46, 64, 91], dtype=np.int32)
highest = lax.Precision.HIGHEST
MESH = pl.DeviceIdType.MESH
LIMIT = 56 * 1024 * 1024
VMEM = pl.BlockSpec(memory_space=pltpu.VMEM)
SMEM = pl.BlockSpec(memory_space=pltpu.SMEM)


def nt(a, b, precision=None):
    return lax.dot_general(
        a, b, (((1,), (1,)), ((), ())), preferred_element_type=F32, precision=precision
    )


def tn(a, b, precision=None):
    return lax.dot_general(
        a, b, (((0,), (0,)), ((), ())), preferred_element_type=F32, precision=precision
    )


def nn(a, b, precision=None):
    return jnp.dot(a, b, preferred_element_type=F32, precision=precision)


def call(kernel, outs, args, scratch=(), collective=None, specs=None):
    params = dict(vmem_limit_bytes=LIMIT)
    if collective is not None:
        params.update(collective_id=collective, has_side_effects=True)
    return pl.pallas_call(
        kernel,
        out_shape=[jax.ShapeDtypeStruct(s, d) for s, d in outs],
        in_specs=specs or [VMEM] * len(args),
        out_specs=[VMEM] * len(outs),
        scratch_shapes=list(scratch),
        compiler_params=pltpu.CompilerParams(**params),
    )(*args)


def greet(peers):
    barrier = pltpu.get_barrier_semaphore()
    for peer in peers:
        pl.semaphore_signal(barrier, inc=1, device_id=peer, device_id_type=MESH)


def meet(peers):
    pl.semaphore_wait(pltpu.get_barrier_semaphore(), len(peers))


def enter(peers):
    greet(peers)
    meet(peers)


def remote(src, dst, send, recv, peer):
    copy = pltpu.make_async_remote_copy(
        src_ref=src, dst_ref=dst, send_sem=send, recv_sem=recv, device_id=peer, device_id_type=MESH
    )
    copy.start()
    return copy


def ring(axis, size):
    me = lax.axis_index(axis)
    return [lax.rem(me + k, size) for k in range(1, size)]


def group_peers(n_exp, n_col):
    n = n_exp * n_col
    me = lax.axis_index("exp") * n_col + lax.axis_index("col")
    return [lax.rem(me + k, n) for k in range(1, n)]


def bias_grid(rel_row, size):
    x = jnp.broadcast_to(rel_row, (size, 2 * size))
    return pltpu.roll(x, size + 1, 1, stride=1, stride_axis=0)[:, :size]


def head_probs(q, k, bias, length):
    scores = nt(q, k) * DH ** (-0.5) + bias
    key_at = lax.broadcasted_iota(jnp.int32, (1, k.shape[0]), 1)
    scores = jnp.where(key_at < length, scores, -1e30)
    top = jnp.max(scores, axis=-1, keepdims=True)
    raised = jnp.exp(scores - top)
    return raised * (1.0 / jnp.sum(raised, axis=-1, keepdims=True))


def eye(size, dtype=BF16):
    return jnp.where(
        lax.broadcasted_iota(jnp.int32, (size, size), 0)
        == lax.broadcasted_iota(jnp.int32, (size, size), 1),
        1.0,
        0.0,
    ).astype(dtype)


def forward_kernel(
    n_exp, n_col, n_row,
    length, tok, w_own, out_own, gain_one, gain_two, router, table, picks,
    w, hid, qkv, heads, out, vectors, rel,
    bias, x, held, small, small_all, w_all, o_own, o_all,
    send, recv, send2, recv2, s_w, r_w, s_o, r_o, s_s, r_s, c_w, d_w, c_o, d_o, c_s, d_s,
):
    e = lax.axis_index("exp")
    c = lax.axis_index("col")
    r = lax.axis_index("row")
    peers = ring("row", n_row)
    exps = ring("exp", n_exp)
    other = {"col": 1 - c}
    everyone = [{"row": p} for p in peers] + [{"exp": p} for p in exps] + [other]
    greet(everyone)
    size = tok.shape[0]
    block = size // n_row
    local = qkv.shape[2]
    shard = w_own.shape[1]
    experts = router.shape[1]
    small[...] = jnp.zeros(small.shape, F32)
    small[0:experts, 0:shard] = tn(router[...], eye(shard))
    small[experts : experts + 1, 0:shard] = gain_one[...].astype(F32)
    small[experts + 1 : experts + 2, 0:shard] = gain_two[...].astype(F32)
    o_own[...] = nt(eye(shard), out_own[...]).astype(BF16)
    small_all[e, c] = small[...]
    w_all[e, c] = w_own[...]
    o_all[e, c] = o_own[...]
    meet(everyone)
    gathers = [
        (small, small_all, s_s, r_s, c_s, d_s),
        (w_own, w_all, s_w, r_w, c_w, d_w),
        (o_own, o_all, s_o, r_o, c_o, d_o),
    ]
    first = [
        [
            remote(own, full.at[e, c], a.at[k], b.at[k], {"exp": p})
            for own, full, a, b, _, _ in gathers
        ]
        for k, p in enumerate(exps)
    ]
    second = [
        [remote(own, full.at[e, c], a.at[0], b.at[0], other)] for own, full, _, _, a, b in gathers
    ]

    def forward_on(which):
        _, full, _, _, a, b = gathers[which]
        for k in range(n_exp - 1):
            q = lax.rem(e + n_exp - k - 1, n_exp)
            first[k][which].wait_recv()
            at = full.at[q, c]
            second[which].append(remote(at, at, a.at[k + 1], b.at[k + 1], other))

    rel[...] = tn(table[...], picks[...])
    for h in range(local // DH):
        bias[h] = bias_grid(rel[h : h + 1], size)
    rows_in = tok[...].astype(F32)
    inv = lax.rsqrt(jnp.mean(rows_in * rows_in, axis=-1, keepdims=True) + epsilon)
    forward_on(0)
    forward_on(1)
    for which in range(2):
        for copy in second[which]:
            copy.wait_recv()
    for k in range(n_exp * n_col):
        at = slice(k * shard, (k + 1) * shard)
        vectors[:, at] = small_all[k // n_col, k % n_col][:, :shard]
        if shard % 16 == 0:
            w[0:3, at] = w_all[k // n_col, k % n_col]
    if shard % 16:
        pieces = [
            w_all[k // n_col, k % n_col].astype(F32) for k in range(n_exp * n_col)
        ]
        w[0:3] = jnp.concatenate(pieces, axis=1).astype(BF16)
    hid[...] = (rows_in * inv * vectors[experts : experts + 1]).astype(BF16)
    for m in range(3):
        qkv[m] = nn(hid[...], w[m]).astype(BF16)
    forward_on(2)
    copies = []
    for k, p in enumerate(peers + [r]):
        rows = pl.ds(pl.multiple_of(p * block, block), block)
        for h in range(local // DH):
            at = slice(h * DH, (h + 1) * DH)
            probs = head_probs(qkv[0, rows, at], qkv[1, :, at], bias[h, rows], length[0])
            heads[rows, at] = nn(probs.astype(BF16), qkv[2, :, at]).astype(BF16)
        if k == 0:
            for copy in second[2]:
                copy.wait_recv()
            if shard % 16:
                pieces = [
                    o_all[j // n_col, j % n_col].astype(F32) for j in range(n_exp * n_col)
                ]
                w[3] = jnp.concatenate(pieces, axis=0).astype(BF16)
            else:
                for j in range(n_exp * n_col):
                    w[3, j * shard : (j + 1) * shard] = o_all[j // n_col, j % n_col]
        x[k] = nt(heads[rows, :], w[3]).astype(BF16)
        if k < n_row - 1:
            copies.append(remote(x.at[k], held.at[k], send.at[k], recv.at[k], {"row": p}))
    total = x[n_row - 1].astype(F32)
    for k, copy in enumerate(copies):
        copy.wait_recv()
        total = total + held[k].astype(F32)
    out[r] = total.astype(BF16)
    more = [
        remote(out.at[r], out.at[r], send2.at[k], recv2.at[k], {"row": p})
        for k, p in enumerate(peers)
    ]
    for copy in copies + sum(first, []) + sum(second, []):
        copy.wait_send()
    for copy in more:
        copy.wait()


def middle(length, tok, attn, vectors, experts, route_row):
    size = tok.shape[0]
    mixed = tok[...].astype(F32) + attn[...].astype(F32)
    inv = lax.rsqrt(jnp.mean(mixed * mixed, axis=-1, keepdims=True) + epsilon)
    unit = mixed * inv
    hidden = (unit * vectors[experts + 1 : experts + 2]).astype(BF16)
    logits = nt(hidden, vectors[0:experts].astype(BF16))
    top = jnp.max(logits, axis=-1, keepdims=True)
    raised = jnp.exp(logits - top)
    probs = raised / jnp.sum(raised, axis=-1, keepdims=True)
    live = lax.broadcasted_iota(jnp.int32, (1, size), 1) < length
    chosen = lax.broadcasted_iota(jnp.int32, (experts, size), 0) == route_row[...]
    chosen = jnp.where(chosen, 1.0, 0.0)
    hot_col = tn(chosen.astype(BF16), eye(experts))
    gate = jnp.sum(hot_col * probs, axis=-1, keepdims=True)
    hot = jnp.where(live, chosen, 0.0)
    earlier = jnp.where(
        lax.broadcasted_iota(jnp.int32, (size, size), 0)
        < lax.broadcasted_iota(jnp.int32, (size, size), 1),
        1.0,
        0.0,
    )
    before = nn(hot.astype(BF16), earlier.astype(BF16))
    rank = jnp.sum(hot * before, axis=0, keepdims=True).astype(jnp.int32)
    kept = live & (rank < CAP)
    target = jnp.where(kept, route_row[...] * CAP + rank, -1)
    match = lax.broadcasted_iota(jnp.int32, (experts * CAP, size), 0) == target
    match = jnp.where(match, 1.0, 0.0).astype(BF16)
    return mixed, inv, unit, hidden, probs, hot_col, gate, match


def expert_kernel(
    n_exp, n_col, n_row, experts,
    length, tok, attn, vectors, route_row, cot, w_in, w_out,
    out, rows, grads, acted, grad_before,
    sent, arrived, part, held, total, sums, s_a, r_a, s_b, r_b, s_c, r_c, s_d, r_d,
):
    n = n_exp * n_col
    r = lax.axis_index("row")
    me = lax.axis_index("exp") * n_col + lax.axis_index("col")
    peers = ring("row", n_row)
    group = group_peers(n_exp, n_col)
    ids = [{"exp": p // n_col, "col": lax.rem(p, n_col)} for p in group]
    everyone = [{"row": p} for p in peers] + ids
    greet(everyone)
    _, _, _, hidden, _, _, gate, match = middle(
        length[0], tok, attn, vectors, experts, route_row
    )
    grad = (gate * cot[...].astype(F32)).astype(BF16)
    first = nn(match, hidden).reshape(n, CAP, -1)
    second = nn(match, grad).reshape(n, CAP, -1)
    sent[...] = jnp.concatenate([first, second], axis=1).astype(BF16)
    meet(everyone)
    copies = [
        remote(sent.at[p], arrived.at[me], s_a.at[k], r_a.at[k], ids[k]) for k, p in enumerate(group)
    ]
    arrived[me] = sent[me]
    for copy in copies:
        copy.wait()
    both = arrived[...].astype(F32)
    rows[...] = both[:, :CAP].reshape(n * CAP, -1).astype(BF16)
    grads[...] = both[:, CAP:].reshape(n * CAP, -1).astype(BF16)
    before = nn(rows[...], w_in[0])
    scale = np.float32(np.sqrt(2 / np.pi))
    inner = jnp.tanh(scale * (before + 0.044715 * before * before * before))
    acted[...] = (0.5 * before * (1.0 + inner)).astype(BF16)
    slope = 0.5 * (1.0 + inner) + 0.5 * before * (1.0 - inner * inner) * scale * (
        1.0 + 3 * 0.044715 * before * before
    )
    result = nn(acted[...], w_out[0])
    grad_before[...] = (slope * nt(grads[...], w_out[0])).astype(BF16)
    back = nt(grad_before[...], w_in[0])
    both = jnp.concatenate([result.reshape(n, CAP, -1), back.reshape(n, CAP, -1)], axis=1)
    wide = both.shape[2] // n_row
    for b in range(n_row):
        part[b] = both[:, :, b * wide : (b + 1) * wide].astype(BF16)
    copies = [
        remote(part.at[p], held.at[k], s_b.at[k], r_b.at[k], {"row": p}) for k, p in enumerate(peers)
    ]
    acc = part[r].astype(F32)
    for k, copy in enumerate(copies):
        copy.wait_recv()
        acc = acc + held[k].astype(F32)
    total[...] = acc.astype(BF16)
    copies += [
        remote(total.at[p], sums.at[me], s_c.at[k], r_c.at[k], ids[k]) for k, p in enumerate(group)
    ]
    sums[me] = total[me]
    for copy in copies[n_row - 1 :]:
        copy.wait_recv()
    out[r] = sums[...]
    last = [
        remote(sums, out.at[r], s_d.at[k], r_d.at[k], {"row": p}) for k, p in enumerate(peers)
    ]
    for copy in copies:
        copy.wait_send()
    for copy in last:
        copy.wait()


def output_kernel(
    experts, rows, grads, acted, grad_before, result_in, gt_in, gwo, smo,
    result, gt, g_qkv, g_out, g_table, g_one, g_two, g_router, grad_in, grad_out,
):
    grad_in[0] = tn(rows[...], grad_before[...])
    grad_out[0] = tn(acted[...], grads[...])
    result[...] = result_in[...]
    for b in range(gt_in.shape[0]):
        block = gt_in.shape[1]
        gt[b * block : (b + 1) * block] = gt_in[b]
    g_qkv[...] = gwo[0:3]
    g_out[...] = gwo[3].T
    shard = gwo.shape[1]
    lines = experts + 2
    g_table[...] = smo[lines : lines + g_table.shape[1], : g_table.shape[0]].T
    g_one[...] = smo[experts + 1 : experts + 2, :shard]
    g_two[...] = smo[experts : experts + 1, :shard]
    g_router[...] = smo[0:experts, :shard]


def backward_kernel(
    n_exp, n_col, n_row, experts,
    length, tok, attn, vectors, route_row, cot, back_parts, hid, qkv, heads, w, rel, picks,
    result, gt, gwo, smo,
    gproj, gw, gm, gh, sm, hrow, sib, pre, zheld, smheld, smrow, go, sib_o, pre_o, zheld_o,
    s_row, r_row, s_row2, r_row2, s_sib, r_sib, s_z, r_z, s_sm, r_sm, s_sm2, r_sm2, s_so, r_so, s_zo, r_zo,
):
    e = lax.axis_index("exp")
    c = lax.axis_index("col")
    r = lax.axis_index("row")
    n = n_exp * n_col
    me = e * n_col + c
    rows = ring("row", n_row)
    exps = ring("exp", n_exp)
    group = group_peers(n_exp, n_col)
    ids = [{"exp": p // n_col, "col": lax.rem(p, n_col)} for p in group]
    everyone = [{"row": p} for p in rows] + ids
    greet(everyone)
    size, width = tok.shape
    block = size // n_row
    shard = width // n
    local = qkv.shape[2]

    def place(m, grad):
        for k in range(n):
            piece = grad[k * shard : (k + 1) * shard].astype(BF16)
            if m == 3:
                go[k % n_col, k // n_col] = piece
            else:
                gw[k % n_col, k // n_col, m] = piece

    mixed, inv, unit, hidden, probs, hot_col, gate, match = middle(
        length[0], tok, attn, vectors, experts, route_row
    )
    both = jnp.concatenate([back_parts[b].astype(F32) for b in range(n_row)], axis=-1)
    router = vectors[0:experts].astype(BF16)
    gain_one = vectors[experts : experts + 1]
    gain_two = vectors[experts + 1 : experts + 2]
    out_rows = both[:, :CAP].reshape(n * CAP, -1).astype(BF16)
    back_rows = both[:, CAP:].reshape(n * CAP, -1).astype(BF16)
    expert_result = tn(match, out_rows)
    upstream = cot[...].astype(F32)
    result[...] = (mixed + gate * expert_result).astype(BF16)
    grad_gate = jnp.sum(upstream * expert_result, axis=-1, keepdims=True)
    grad_logits = probs * (hot_col * grad_gate - gate * grad_gate)
    grad_low = grad_logits.astype(BF16)
    grad_rest = (grad_logits - grad_low.astype(F32)).astype(BF16)
    grad_router = tn(grad_low, hidden) + tn(grad_rest, hidden)
    grad_hidden = tn(match, back_rows) + nn(grad_low, router) + nn(grad_rest, router)
    grad_gain_two = jnp.sum(grad_hidden * unit, axis=0, keepdims=True)
    scaled = grad_hidden * gain_two
    gm[...] = upstream + inv * (scaled - unit * jnp.mean(scaled * unit, axis=-1, keepdims=True))
    gattn = gm[...].astype(BF16)
    place(3, tn(gattn, heads[...]))
    meet(everyone)
    sibling_o = remote(go.at[1 - c], sib_o, s_so, r_so, {"col": 1 - c})
    grad_heads = nn(gattn, w[3]).astype(BF16)
    flip = jnp.where(
        lax.broadcasted_iota(jnp.int32, (size, size), 0)
        + lax.broadcasted_iota(jnp.int32, (size, size), 1)
        == size - 1,
        1.0,
        0.0,
    ).astype(BF16)
    sm[...] = jnp.zeros(sm.shape, F32)
    lines = experts + 2
    for h in range(local // DH):
        at = slice(h * DH, (h + 1) * DH)
        q, k, v = qkv[0, :, at], qkv[1, :, at], qkv[2, :, at]
        probs_full = head_probs(q, k, bias_grid(rel[h : h + 1], size), length[0])
        gheads = grad_heads[:, at]
        gprobs = nt(gheads, v)
        dot = jnp.sum(probs_full * gprobs, axis=-1, keepdims=True)
        gscores = (probs_full * (gprobs - dot)).astype(BF16)
        gproj[2, :, at] = tn(probs_full.astype(BF16), gheads).astype(BF16)
        gproj[0, :, at] = (nn(gscores, k) * DH ** (-0.5)).astype(BF16)
        gproj[1, :, at] = (tn(gscores, q) * DH ** (-0.5)).astype(BF16)
        turned = nn(flip, gscores)
        turned = jnp.concatenate([turned, jnp.zeros((size, size), F32)], axis=1)
        turned = pltpu.roll(turned, 0, 1, stride=1, stride_axis=0)
        diagonal = jnp.sum(turned, axis=0, keepdims=True)
        line = nt(diagonal, picks[...].astype(F32), highest)
        for k in range(n):
            sm[k, lines + h : lines + h + 1, 0 : line.shape[1]] = line
    sibling_o.wait_recv()
    pre_o[...] = (go[c].astype(F32) + sib_o[...].astype(F32)).astype(BF16)
    z_copies_o = [
        remote(pre_o.at[p], zheld_o.at[k], s_zo.at[k], r_zo.at[k], {"exp": p})
        for k, p in enumerate(exps)
    ]
    row_copies = []
    grad_gain_one = jnp.zeros((1, width), F32)
    for k, p in enumerate(rows + [r]):
        at = pl.ds(pl.multiple_of(p * block, block), block)
        ghid = nt(gproj[0, at, :], w[0]) + nt(gproj[1, at, :], w[1]) + nt(gproj[2, at, :], w[2])
        rows_in = tok[at, :].astype(F32)
        inv_one = lax.rsqrt(jnp.mean(rows_in * rows_in, axis=-1, keepdims=True) + epsilon)
        unit_one = rows_in * inv_one
        grad_gain_one = grad_gain_one + jnp.sum(ghid * unit_one, axis=0, keepdims=True)
        if k < n_row - 1:
            gh[k] = ghid.astype(BF16)
            row_copies.append(remote(gh.at[k], hrow.at[k], s_row.at[k], r_row.at[k], {"row": p}))
    for m in range(3):
        place(m, tn(hid[...], gproj[m]))
    sibling = remote(gw.at[1 - c], sib, s_sib, r_sib, {"col": 1 - c})
    for k in range(n):
        at = slice(k * shard, (k + 1) * shard)
        sm[k, 0:experts, 0:shard] = grad_router[:, at]
        sm[k, experts : experts + 1, 0:shard] = grad_gain_two[:, at]
        sm[k, experts + 1 : experts + 2, 0:shard] = grad_gain_one[:, at]
    small = [
        remote(sm.at[p], smheld.at[k], s_sm.at[k], r_sm.at[k], ids[k]) for k, p in enumerate(group)
    ]
    sibling.wait_recv()
    pre[...] = (gw[c].astype(F32) + sib[...].astype(F32)).astype(BF16)
    z_copies = [
        remote(pre.at[p], zheld.at[k], s_z.at[k], r_z.at[k], {"exp": p}) for k, p in enumerate(exps)
    ]
    total = ghid
    for k, copy in enumerate(row_copies):
        copy.wait_recv()
        total = total + hrow[k].astype(F32)
    scaled = total * gain_one
    own = pl.ds(pl.multiple_of(r * block, block), block)
    gt[r] = (
        gm[own, :]
        + inv_one * (scaled - unit_one * jnp.mean(scaled * unit_one, axis=-1, keepdims=True))
    ).astype(BF16)
    row_copies2 = [
        remote(gt.at[r], gt.at[r], s_row2.at[k], r_row2.at[k], {"row": p}) for k, p in enumerate(rows)
    ]
    part = sm[me]
    for k, copy in enumerate(small):
        copy.wait_recv()
        part = part + smheld[k]
    smrow[0] = part
    small2 = [
        remote(smrow.at[0], smrow.at[k + 1], s_sm2.at[k], r_sm2.at[k], {"row": p})
        for k, p in enumerate(rows)
    ]
    full = part
    for k, copy in enumerate(small2):
        copy.wait_recv()
        full = full + smrow[k + 1]
    row_at = lax.broadcasted_iota(jnp.int32, part.shape, 0)
    smo[...] = jnp.where(row_at == experts + 1, full, part)
    wsum = pre[e].astype(F32)
    for k, copy in enumerate(z_copies):
        copy.wait_recv()
        wsum = wsum + zheld[k].astype(F32)
    gwo[0:3] = wsum
    osum = pre_o[e].astype(F32)
    for k, copy in enumerate(z_copies_o):
        copy.wait_recv()
        osum = osum + zheld_o[k].astype(F32)
    gwo[3] = osum
    for copy in [sibling, sibling_o] + z_copies_o + row_copies + small + z_copies + small2:
        copy.wait_send()
    for copy in row_copies2:
        copy.wait()


def bucket_picks(length, buckets):
    offset = np.arange(2 * length) - (length - 1)
    distance = np.abs(offset)
    beyond = np.sum(distance[:, None] >= thresholds, axis=-1)
    bucket = (offset > 0) * 16 + np.minimum(distance, 8) + beyond
    return (bucket[:, None] == np.arange(buckets)[None, :]).astype(np.float32)


def body(
    n_exp, n_col, n_row,
    tokens, qkv_weight, out_weight, bias_table, gain_attn, gain_expert, router_weight,
    expert_in, expert_out, lengths, routes, cotangent,
):
    n = n_exp * n_col
    size, width = tokens.shape
    shard = width // n
    local = qkv_weight.shape[2]
    heads_local = local // DH
    experts = router_weight.shape[1]
    lines = -(-(experts + 2) // 16) * 16
    dma = lambda k: pltpu.SemaphoreType.DMA((k,))
    picks = jnp.asarray(bucket_picks(size, bias_table.shape[0]).T, BF16)
    route_row = routes.reshape(1, size)
    block = size // n_row
    w, hid, qkv, heads, attn, vectors, rel = call(
        functools.partial(forward_kernel, n_exp, n_col, n_row),
        [
            ((4, width, local), BF16),
            ((size, width), BF16),
            ((3, size, local), BF16),
            ((size, local), BF16),
            ((n_row, block, width), BF16),
            ((lines, width), F32),
            ((heads_local, 2 * size), F32),
        ],
        [
            lengths, tokens, qkv_weight, out_weight, gain_attn.reshape(1, shard),
            gain_expert.reshape(1, shard), router_weight, bias_table, picks,
        ],
        [
            pltpu.VMEM((heads_local, size, size), F32),
            pltpu.VMEM((n_row, block, width), BF16),
            pltpu.VMEM((n_row - 1, block, width), BF16),
            pltpu.VMEM((lines, 128), F32),
            pltpu.VMEM((n_exp, n_col, lines, 128), F32),
            pltpu.VMEM((n_exp, n_col, 3, shard, local), BF16),
            pltpu.VMEM((shard, local), BF16),
            pltpu.VMEM((n_exp, n_col, shard, local), BF16),
        ]
        + [dma(n_row - 1)] * 4
        + [dma(n_exp - 1)] * 6
        + [dma(n_exp)] * 6,
        2,
        specs=[SMEM] + [VMEM] * 8,
    )
    attn = attn.reshape(size, width)
    slots = pltpu.VMEM((n, 2 * CAP, width), BF16)
    wide = width // n_row
    back, *saved = call(
        functools.partial(expert_kernel, n_exp, n_col, n_row, experts),
        [
            ((n_row, n, 2 * CAP, wide), BF16),
            ((n * CAP, width), BF16),
            ((n * CAP, width), BF16),
            ((n * CAP, expert_in.shape[2]), BF16),
            ((n * CAP, expert_in.shape[2]), BF16),
        ],
        [lengths, tokens, attn, vectors, route_row, cotangent, expert_in, expert_out],
        [
            slots, slots,
            pltpu.VMEM((n_row, n, 2 * CAP, wide), BF16),
            pltpu.VMEM((n_row - 1, n, 2 * CAP, wide), BF16),
            pltpu.VMEM((n, 2 * CAP, wide), BF16),
            pltpu.VMEM((n, 2 * CAP, wide), BF16),
            dma(n - 1), dma(n - 1), dma(n_row - 1), dma(n_row - 1),
            dma(n - 1), dma(n - 1), dma(n_row - 1), dma(n_row - 1),
        ],
        3,
        specs=[SMEM] + [VMEM] * 7,
    )
    high = -(-(experts + 2 + heads_local) // 8) * 8
    result, gt, gwo, smo = call(
        functools.partial(backward_kernel, n_exp, n_col, n_row, experts),
        [
            ((size, width), BF16),
            ((n_row, block, width), BF16),
            ((4, shard, local), F32),
            ((high, 128), F32),
        ],
        [
            lengths, tokens, attn, vectors, route_row, cotangent, back, hid, qkv, heads, w, rel,
            picks,
        ],
        [
            pltpu.VMEM((3, size, local), BF16),
            pltpu.VMEM((n_col, n_exp, 3, shard, local), BF16),
            pltpu.VMEM((size, width), F32),
            pltpu.VMEM((n_row - 1, block, width), BF16),
            pltpu.VMEM((n, high, 128), F32),
            pltpu.VMEM((n_row - 1, block, width), BF16),
            pltpu.VMEM((n_exp, 3, shard, local), BF16),
            pltpu.VMEM((n_exp, 3, shard, local), BF16),
            pltpu.VMEM((n_exp - 1, 3, shard, local), BF16),
            pltpu.VMEM((n - 1, high, 128), F32),
            pltpu.VMEM((n_row, high, 128), F32),
            pltpu.VMEM((n_col, n_exp, shard, local), BF16),
            pltpu.VMEM((n_exp, shard, local), BF16),
            pltpu.VMEM((n_exp, shard, local), BF16),
            pltpu.VMEM((n_exp - 1, shard, local), BF16),
            dma(n_row - 1), dma(n_row - 1), dma(n_row - 1), dma(n_row - 1),
            pltpu.SemaphoreType.DMA, pltpu.SemaphoreType.DMA,
            dma(n_exp - 1), dma(n_exp - 1),
            dma(n - 1), dma(n - 1), dma(n_row - 1), dma(n_row - 1),
            pltpu.SemaphoreType.DMA, pltpu.SemaphoreType.DMA,
            dma(n_exp - 1), dma(n_exp - 1),
        ],
        4,
        specs=[SMEM] + [VMEM] * 12,
    )
    (
        result, gt, g_qkv, g_out, g_table, g_one, g_two, g_router, grad_in, grad_out,
    ) = call(
        functools.partial(output_kernel, experts),
        [
            ((size, width), BF16),
            ((size, width), BF16),
            (qkv_weight.shape, F32),
            (out_weight.shape, F32),
            (bias_table.shape, F32),
            ((1, shard), F32),
            ((1, shard), F32),
            ((experts, shard), F32),
            (expert_in.shape, F32),
            (expert_out.shape, F32),
        ],
        [*saved, result, gt, gwo, smo],
    )
    return (
        result, gt, g_qkv, g_out, g_table, g_one.reshape(shard), g_two.reshape(shard), g_router.T,
        grad_in, grad_out,
    )


def solution(mesh):
    both = ("exp", "col")
    placed = (
        P(both, None),
        P(None, both, "row"),
        P("row", both),
        P(None, "row"),
        P(both),
        P(both),
        P(both, None),
        P(both, None, "row"),
        P(both, "row", None),
        P(both),
        P(both, None),
        P(both, None),
    )
    shape = mesh.shape
    return jax.shard_map(
        functools.partial(body, shape["exp"], shape["col"], shape["row"]),
        mesh=mesh,
        in_specs=placed,
        out_specs=(
            P(both, None),
            P(both, None),
            P(None, both, "row"),
            P("row", both),
            P(None, "row"),
            P(both),
            P(both),
            P(both, None),
            P(both, None, "row"),
            P(both, "row", None),
        ),
        check_vma=False,
    )
```
